256 devices in a mesh: ctx: 64 (over z, x_lo, y), kvh: 4 (over x_hi, core).
Axes of the slice: x: 4 (x_hi: 2, x_lo: 2; x = x_hi * 2 + x_lo), y: 4, z: 8, core: 2. Of those that a mesh axis runs over, the one named last changes fastest.
Arguments:
- queries: bfloat16 [16384, 64, 128], P('ctx', 'kvh'), may hold values from -16 to 16
- keys: bfloat16 [16384, 4, 128], P('ctx', 'kvh'), may hold values from -8 to 8
- values: bfloat16 [16384, 4, 128], P('ctx', 'kvh'), may hold values from -6 to 6
- doc_ids: int32 [16384], P('ctx'), may hold values from 0 to 127, never falling along the last dimension, each value on 1 to 768 neighbouring positions
Outputs:
- attended: bfloat16 [16384, 8192], P(('ctx', 'kvh'))
The draws below stay inside these ranges and needn't reach their ends.
Inputs may be any that keep to these rules, and one draw needn't show every extreme that they name: doc_ids never falls along the sequence; every document has 1 to 768 positions and one has exactly 768.
All inputs are finite; a program needn't handle non-finite values.
Results may differ from the reference program's by a relative error of at most 0.0039.
Values may be sent and summed in bfloat16 or wider, within the bound.
A program may use at most 64 MiB of HBM per device.

```python
import math
import jax
import jax.numpy as jnp
import numpy as np
from jax import lax

HEAD_WIDTH = 128
HQ = 64
LOCAL_KEY_HEADS = 4
QUERY_GROUP_SIZE = 16
STEPS = 4
SHARD_TOKENS = 256
TOKEN_COUNT = 16384
MOST = 768
DOCS = 128
N_CTX = 64


def draw_queries(key, part):
    key = jax.random.fold_in(key, 11)
    base_offset = jnp.clip(jax.random.normal(key, (TOKEN_COUNT, HQ, HEAD_WIDTH), jnp.float32), -4.0, 4.0)
    return base_offset.astype(jnp.bfloat16)


def draw_keys(key, part):
    key = jax.random.fold_in(key, 23)
    base_offset = jnp.clip(jax.random.normal(key, (TOKEN_COUNT, LOCAL_KEY_HEADS, HEAD_WIDTH), jnp.float32), -4.0, 4.0)
    return base_offset.astype(jnp.bfloat16)


def block_scale(key, dims, cuts, smallest, top_value):
    factor_of = 1.0
    for axis_at, parts in cuts:
        steps = jax.random.uniform(jax.random.fold_in(jax.random.fold_in(key, 6), axis_at), (parts,), jnp.float32, smallest / len(cuts), top_value / len(cuts))
        factor_of = factor_of * jnp.repeat(jnp.exp(steps), dims[axis_at] // parts).reshape((-1,) + (1,) * (len(dims) - 1 - axis_at))
    return factor_of


def profile(number_of, total, most, lean):
    weights = [(1 << 20) // math.isqrt(rank ** lean) + 1 for rank in range(2, number_of + 1)]
    spare, holding = total - most - (number_of - 1), [1] * (number_of - 1)
    while spare > 0:
        free = [i for i in range(number_of - 1) if holding[i] < most]
        whole, remaining = sum([weights[i] for i in free]), spare
        for i in free:
            extra = min(most - holding[i], max(1, remaining * weights[i] // whole), spare)
            holding[i] = holding[i] + extra
            spare = spare - extra
    return np.array([most] + holding)


def ragged_sizes(rng, amount, total, most, lean):
    if amount == 2:
        one = jax.random.randint(rng, (), max(1, total - most), min(most, total - 1) + 1)
        return jnp.stack([one, total - one])
    lengths = jnp.asarray(profile(amount, total, most, lean), jnp.int32)
    pairs = (amount - 1) // 2
    donor, taker = lengths[1:1 + 2 * pairs:2], lengths[2:2 + 2 * pairs:2]
    room = jnp.minimum(donor - 1, most - taker)
    moved = jax.random.randint(jax.random.fold_in(rng, 1), (pairs,), 0, 1 << 20) % (room + 1)
    lengths = lengths.at[1:1 + 2 * pairs:2].set(donor - moved).at[2:2 + 2 * pairs:2].set(taker + moved)
    return lengths[jax.random.permutation(jax.random.fold_in(rng, 2), amount)]


def bell_draw(stream_key, shape, scale, most, split=(), kind=jnp.bfloat16):
    values = jax.random.normal(stream_key, shape, jnp.float32) * scale
    if len(split) > 0:
        values = block_scale(stream_key, shape, split, -0.22, 0.18) * values
    return jnp.clip(values, min=-most, max=most).astype(kind)


def setup_inputs(seed: int = 0) -> dict:
    streams_of = jax.random.split(jax.random.key(seed), 5)
    return {
        "queries": draw_queries(jax.random.fold_in(streams_of[4], 71), 0),
        "keys": draw_keys(jax.random.fold_in(streams_of[4], 71), 0),
        "values": bell_draw(streams_of[2], (TOKEN_COUNT, LOCAL_KEY_HEADS, HEAD_WIDTH), 1.0, 6.0, ((0, 64), (1, 4))),
        "doc_ids": jnp.searchsorted(jnp.cumsum(ragged_sizes(streams_of[3], DOCS, TOKEN_COUNT, MOST, 2)), jnp.arange(TOKEN_COUNT), side="right").astype(jnp.int32),
    }


def reference(queries, keys, values, doc_ids):
    scale = 1.0 / (HEAD_WIDTH ** 0.5)
    offsets = jnp.arange(SHARD_TOKENS, dtype=jnp.int32)
    window = jnp.arange(STEPS * SHARD_TOKENS, dtype=jnp.int32)

    def one_shard(shard):
        start_index = (shard * SHARD_TOKENS).astype(jnp.int32)
        query_block = lax.dynamic_slice_in_dim(queries, start_index, SHARD_TOKENS, 0).reshape(SHARD_TOKENS, LOCAL_KEY_HEADS, QUERY_GROUP_SIZE, HEAD_WIDTH)
        query_ids = lax.dynamic_slice_in_dim(doc_ids, start_index, SHARD_TOKENS, 0)
        query_pos = start_index + offsets
        index = ((start_index - (STEPS - 1) * SHARD_TOKENS + window) % TOKEN_COUNT).astype(jnp.int32)
        key_blk = keys[index]
        value_blk = values[index]
        key_ids = doc_ids[index]
        allowed = (query_ids[:, None] == key_ids[None, :]) & (index[None, :] <= query_pos[:, None])
        score = jnp.einsum("qhgd,khd->hgqk", query_block.astype(jnp.float32), key_blk.astype(jnp.float32)) * scale
        score = jnp.where(allowed, score, -jnp.inf)
        top = jnp.max(score, axis=-1, keepdims=True)
        weight = jnp.exp(score - top)
        total = jnp.sum(weight, axis=-1)
        rounded = lax.optimization_barrier(weight.astype(jnp.bfloat16))
        summed = jnp.einsum("hgqk,khd->hgqd", rounded.astype(jnp.float32), value_blk.astype(jnp.float32))
        result = summed / total[..., None]
        return result.transpose(2, 0, 1, 3).reshape(SHARD_TOKENS, HQ * HEAD_WIDTH).astype(jnp.bfloat16)

    blocks = lax.map(one_shard, jnp.arange(N_CTX, dtype=jnp.int32))
    return blocks.reshape(TOKEN_COUNT, HQ * HEAD_WIDTH)
```

```python
import functools

import jax
import jax.numpy as jnp
from jax import lax
from jax.experimental import pallas as pl
from jax.experimental.pallas import tpu as pltpu
from jax.sharding import PartitionSpec as P

MESH = pl.DeviceIdType.MESH
BACK = 3
SHARD = 256
GROUP = 16
WIDTH = 128
KEYS = (BACK + 1) * SHARD
BLOCK = 64
WINDOW = BACK * SHARD + BLOCK
TILE = 64
PIECES = BLOCK // TILE
ROWS = TILE * GROUP
HIDE = -131072.0
EXP2 = 1.4426950408889634 / WIDTH**0.5
LAST = (((1,), (1,)), ((), ()))
PLAIN = (((1,), (0,)), ((), ()))


def kernel(
    q_hbm, k_hbm, v_hbm, ids_hbm, out_hbm,
    q_buf, k_buf, v_buf, id_buf, pick, bias, stage, turned,
    load_sem, kv_send, kv_recv, out_send, out_recv, own_sem,
):
    ctx = lax.axis_index("ctx")
    kvh = lax.axis_index("kvh")
    shards = lax.axis_size("ctx")
    pair, core = kvh // 2, kvh % 2

    def behind(by):
        return (lax.rem(ctx + shards - by, shards), kvh)

    def ahead(by):
        return (lax.rem(ctx + by, shards), kvh)

    def owner(step):
        late, odd = step // 2, step % 2
        x = (1 - pair) * (1 - late) + pair * late
        c = (1 - odd) * (1 - late) + late * ((1 - core) * (1 - odd) + core * odd)
        return 2 * x + c

    barrier = pltpu.get_barrier_semaphore()
    for by in range(1, BACK + 1):
        pl.semaphore_signal(barrier, inc=1, device_id=behind(by), device_id_type=MESH)
    for step in range(3):
        pl.semaphore_signal(barrier, inc=1, device_id=(ctx, owner(step)), device_id_type=MESH)

    own = BACK * SHARD
    loads = [
        pltpu.make_async_copy(ids_hbm, id_buf.at[BACK], load_sem.at[0]),
        pltpu.make_async_copy(k_hbm, k_buf.at[pl.ds(own, SHARD)], load_sem.at[1]),
        pltpu.make_async_copy(v_hbm, v_buf.at[pl.ds(own, SHARD)], load_sem.at[2]),
        pltpu.make_async_copy(q_hbm, q_buf, load_sem.at[3]),
    ]
    for load in loads:
        load.start()

    pl.semaphore_wait(barrier, BACK + 3)
    moves = []
    for by in range(1, BACK + 1):
        to = BACK - by
        rows = pl.ds(to * SHARD, SHARD)
        for i, (src, dst) in enumerate(
            [(ids_hbm, id_buf.at[to]), (k_hbm, k_buf.at[rows]), (v_hbm, v_buf.at[rows])]
        ):
            moves.append(
                pltpu.make_async_remote_copy(
                    src_ref=src, dst_ref=dst, send_sem=kv_send.at[to, i], recv_sem=kv_recv.at[to, i],
                    device_id=ahead(by), device_id_type=MESH,
                )
            )
    for move in moves:
        move.start()

    token = lax.broadcasted_iota(jnp.int32, (SHARD // 2 * GROUP, WIDTH), 0) // GROUP
    lane = lax.broadcasted_iota(jnp.int32, (SHARD // 2 * GROUP, WIDTH), 1)
    pick[...] = jnp.where(token == lane, 1.0, 0.0).astype(jnp.bfloat16)

    def hide(part):
        for r in range(2):
            row = id_buf[part, r : r + 1, :].astype(jnp.float32)
            column = jnp.broadcast_to(row, (WIDTH, WIDTH)).T
            at = part * SHARD + r * WIDTH
            key_pos = lax.broadcasted_iota(jnp.int32, (WIDTH, WIDTH), 0) + at
            query_pos = lax.broadcasted_iota(jnp.int32, (WIDTH, WIDTH), 1) + own
            for half in range(2):
                query = id_buf[BACK, half : half + 1, :].astype(jnp.float32)
                seen = column == query
                if part == BACK:
                    seen = seen & (key_pos <= query_pos + half * WIDTH)
                bias[half, pl.ds(at, WIDTH), :] = jnp.where(seen, 0.0, HIDE).astype(jnp.bfloat16)

    loads[0].wait()
    hide(BACK)
    for i in range(0, len(moves), 3):
        moves[i].wait_recv()
    for part in range(BACK):
        hide(part)
    for load in loads[1:]:
        load.wait()
    for i in range(0, len(moves), 3):
        moves[i + 1].wait_recv()
        moves[i + 2].wait_recv()

    def outgoing(step, piece):
        rows = pl.ds(pl.multiple_of(piece * TILE, TILE), TILE)
        slot = core * (1 - step // 2) + 2 * (step // 2)
        return pltpu.make_async_remote_copy(
            src_ref=stage.at[step, rows],
            dst_ref=out_hbm.at[rows, pl.ds(pl.multiple_of(kvh * GROUP * WIDTH, WIDTH), GROUP * WIDTH)],
            send_sem=out_send.at[step, piece], recv_sem=out_recv.at[slot, piece],
            device_id=(ctx, owner(step)), device_id_type=MESH,
        )

    def kept(piece):
        rows = pl.ds(pl.multiple_of(piece * TILE, TILE), TILE)
        return pltpu.make_async_copy(
            stage.at[3, rows],
            out_hbm.at[rows, pl.ds(pl.multiple_of(kvh * GROUP * WIDTH, WIDTH), GROUP * WIDTH)],
            own_sem.at[piece],
        )

    def work(i, _):
        step, piece = i // PIECES, i % PIECES
        block = owner(step)
        window = pl.ds(pl.multiple_of(block * BLOCK, BLOCK), WINDOW)
        keys = jnp.concatenate([k_buf[window, :], bias[block // 2, window, :]], axis=1)
        ones = jnp.ones((16, WINDOW), jnp.bfloat16)
        values = jnp.concatenate([v_buf[window, :].T, ones], axis=0)
        first = pl.multiple_of((block * PIECES + piece) * ROWS, ROWS)
        inside = pl.multiple_of(((block % 2) * PIECES + piece) * ROWS, ROWS)
        queries = jnp.concatenate([q_buf[pl.ds(first, ROWS), :], pick[pl.ds(inside, ROWS), :]], axis=1)
        score = lax.dot_general(keys, queries, LAST, preferred_element_type=jnp.float32)
        top = jnp.max(score, axis=0, keepdims=True)
        weight = jnp.exp2((score - top) * EXP2).astype(jnp.bfloat16)
        summed = lax.dot_general(values, weight, PLAIN, preferred_element_type=jnp.float32)
        turned[...] = (summed[:WIDTH] / summed[WIDTH : WIDTH + 1]).T
        tokens = pl.ds(pl.multiple_of(piece * TILE, TILE), TILE)
        for head in range(GROUP):
            stage[step, tokens, head * WIDTH : (head + 1) * WIDTH] = turned[
                pl.ds(head, TILE, stride=GROUP), :
            ].astype(jnp.bfloat16)

        @pl.when(step < 3)
        def _():
            outgoing(step, piece).start()

        @pl.when(step == 3)
        def _():
            kept(piece).start()

        return 0

    lax.fori_loop(0, 4 * PIECES, work, 0)

    for move in moves:
        move.wait_send()
    for piece in range(PIECES):
        kept(piece).wait()
        for step in range(3):
            outgoing(step, piece).wait_send()
        for slot in range(3):
            rows = pl.ds(piece * TILE, TILE)
            pltpu.make_async_remote_copy(
                src_ref=stage.at[slot, rows], dst_ref=out_hbm.at[rows, pl.ds(0, GROUP * WIDTH)],
                send_sem=out_send.at[slot, piece], recv_sem=out_recv.at[slot, piece],
                device_id=(ctx, owner(0)), device_id_type=MESH,
            ).wait_recv()


def body(queries, keys, values, doc_ids):
    anywhere = pl.BlockSpec(memory_space=pl.ANY)
    return pl.pallas_call(
        kernel,
        name="attend",
        out_shape=jax.ShapeDtypeStruct((BLOCK, 4 * GROUP * WIDTH), jnp.bfloat16),
        in_specs=[anywhere] * 4,
        out_specs=anywhere,
        scratch_shapes=[
            pltpu.VMEM((SHARD * GROUP, WIDTH), jnp.bfloat16),
            pltpu.VMEM((KEYS, WIDTH), jnp.bfloat16),
            pltpu.VMEM((KEYS, WIDTH), jnp.bfloat16),
            pltpu.VMEM((BACK + 1, 2, WIDTH), jnp.int32),
            pltpu.VMEM((SHARD // 2 * GROUP, WIDTH), jnp.bfloat16),
            pltpu.VMEM((2, KEYS, WIDTH), jnp.bfloat16),
            pltpu.VMEM((4, BLOCK, GROUP * WIDTH), jnp.bfloat16),
            pltpu.VMEM((ROWS, WIDTH), jnp.float32),
            pltpu.SemaphoreType.DMA((4,)),
            pltpu.SemaphoreType.DMA((BACK, 3)),
            pltpu.SemaphoreType.DMA((BACK, 3)),
            pltpu.SemaphoreType.DMA((3, PIECES)),
            pltpu.SemaphoreType.DMA((3, PIECES)),
            pltpu.SemaphoreType.DMA((PIECES,)),
        ],
        compiler_params=pltpu.CompilerParams(
            collective_id=0, has_side_effects=True, vmem_limit_bytes=56 << 20
        ),
        cost_estimate=pl.CostEstimate(
            flops=4 * SHARD * GROUP * KEYS * WIDTH, bytes_accessed=4 << 20, transcendentals=SHARD * GROUP * KEYS
        ),
    )(
        queries.reshape(SHARD * GROUP, WIDTH),
        keys.reshape(SHARD, WIDTH),
        values.reshape(SHARD, WIDTH),
        doc_ids.reshape(2, WIDTH),
    )


def solution(mesh):
    return jax.shard_map(
        body,
        mesh=mesh,
        in_specs=(P("ctx", "kvh", None), P("ctx", "kvh", None), P("ctx", "kvh", None), P("ctx")),
        out_specs=P(("ctx", "kvh"), None),
        check_vma=False,
    )
```

```python
import functools

import jax
import jax.numpy as jnp
from jax import lax
from jax.experimental import pallas as pl
from jax.experimental.pallas import tpu as pltpu
from jax.sharding import PartitionSpec as P

MESH = pl.DeviceIdType.MESH
BACK = 3
RING = 4
CROSS = [(y, by) for y in range(RING) for by in range(1, BACK + 1) if y + by >= RING]
DIRECT = [(1,3),(2,2),(2,3),(3,1)]
PASSED = [flow for flow in CROSS if flow not in DIRECT]
SHARD = 256
GROUP = 16
WIDTH = 128
KEYS = (BACK + 1) * SHARD
BLOCK = 64
WINDOW = BACK * SHARD + BLOCK
TILE = 32
PIECES = BLOCK // TILE
ROWS = TILE * GROUP
HIDE = -131072.0
EXP2 = 1.4426950408889634 / WIDTH**0.5
LAST = (((1,), (1,)), ((), ()))
PLAIN = (((1,), (0,)), ((), ()))


def kernel(
    q_hbm, k_hbm, v_hbm, ids_hbm, out_hbm,
    q_buf, k_buf, v_buf, id_buf, k_pass, v_pass, id_pass, pick, bias, stage, turned,
    load_sem, kv_send, kv_recv, out_send, out_recv, own_sem,
):
    ctx = lax.axis_index("ctx")
    kvh = lax.axis_index("kvh")
    shards = lax.axis_size("ctx")
    pair, core = kvh // 2, kvh % 2

    ring, place = ctx // RING, ctx % RING
    rings = shards // RING

    def any_of(conditions):
        return functools.reduce(jnp.logical_or, conditions, False)

    takes = (ring >= 1) & any_of([place == y for y in sorted({y for y, _ in PASSED})])
    gives = (ring < rings - 1) & any_of([place == y for y in sorted({y for y, _ in PASSED})])
    straight = {by: (place + by < RING) | ((ring < rings - 1) & any_of([place == y for y, b in DIRECT if b == by])) for by in range(1, BACK + 1)}
    reached = {by: (place >= by) | ((ring >= 1) & any_of([place == y + by - RING for y, b in DIRECT if b == by])) for by in range(1, BACK + 1)}
    onward = {by: takes & any_of([place == y for y, b in PASSED if b == by]) for by in range(1, BACK + 1)}
    fed = {by: (ring >= 1) & any_of([place == y + by - RING for y, b in PASSED if b == by]) for by in range(1, BACK + 1)}

    def owner(step):
        late, odd = step // 2, step % 2
        x = (1 - pair) * (1 - late) + pair * late
        c = (1 - odd) * (1 - late) + late * ((1 - core) * (1 - odd) + core * odd)
        return 2 * x + c

    barrier = pltpu.get_barrier_semaphore()
    for by in range(1, BACK + 1):

        @pl.when(reached[by])
        def _():
            pl.semaphore_signal(barrier, inc=1, device_id=(ctx - by, kvh), device_id_type=MESH)

        @pl.when(fed[by])
        def _():
            pl.semaphore_signal(barrier, inc=1, device_id=(ctx - by + RING, kvh), device_id_type=MESH)

    for step in range(3):
        pl.semaphore_signal(barrier, inc=1, device_id=(ctx, owner(step)), device_id_type=MESH)

    @pl.when(takes)
    def _():
        pl.semaphore_signal(barrier, inc=1, device_id=(ctx - RING, kvh), device_id_type=MESH)

    own = BACK * SHARD
    loads = [
        pltpu.make_async_copy(ids_hbm, id_buf.at[BACK], load_sem.at[0]),
        pltpu.make_async_copy(k_hbm, k_buf.at[pl.ds(own, SHARD)], load_sem.at[1]),
        pltpu.make_async_copy(v_hbm, v_buf.at[pl.ds(own, SHARD)], load_sem.at[2]),
        pltpu.make_async_copy(q_hbm, q_buf, load_sem.at[3]),
    ]
    for load in loads:
        load.start()

    sent_to = [gives, *straight.values(), *onward.values()]
    pl.semaphore_wait(barrier, 3 + sum(to.astype(jnp.int32) for to in sent_to))

    def part(i, to):
        if to == BACK + 1:
            return (id_pass, k_pass, v_pass)[i]
        rows = pl.ds(to * SHARD, SHARD)
        return (id_buf.at[to], k_buf.at[rows], v_buf.at[rows])[i]

    def move(i, to, target, passed):
        src = part(i, BACK + 1) if passed else (ids_hbm, k_hbm, v_hbm)[i]
        return pltpu.make_async_remote_copy(
            src_ref=src, dst_ref=part(i, to),
            send_sem=kv_send.at[(to if to <= BACK - 1 else BACK) + (BACK + 1) * passed, i], recv_sem=kv_recv.at[to if to <= BACK - 1 else BACK, i],
            device_id=(target, kvh), device_id_type=MESH,
        )

    @pl.when(gives)
    def _():
        for i in range(3):
            move(i, BACK + 1, ctx + RING, False).start()

    for by in range(1, BACK + 1):

        @pl.when(straight[by])
        def _():
            for i in range(3):
                move(i, BACK - by, ctx + by, False).start()

    for by in range(1, BACK + 1):

        @pl.when(ctx < by)
        def _():
            rows = pl.ds((BACK - by) * SHARD, SHARD)
            id_buf[BACK - by] = jnp.full((2, WIDTH), -1, jnp.int32)
            k_buf[rows] = jnp.zeros((SHARD, WIDTH), jnp.bfloat16)
            v_buf[rows] = jnp.zeros((SHARD, WIDTH), jnp.bfloat16)

    @pl.when(takes)
    def _():
        for i in range(3):
            move(i, BACK + 1, ctx, False).wait_recv()
            for by in range(1, BACK + 1):

                @pl.when(onward[by])
                def _():
                    move(i, BACK - by, ctx + by - RING, True).start()

    token = lax.broadcasted_iota(jnp.int32, (SHARD // 2 * GROUP, WIDTH), 0) // GROUP
    lane = lax.broadcasted_iota(jnp.int32, (SHARD // 2 * GROUP, WIDTH), 1)
    pick[...] = jnp.where(token == lane, 1.0, 0.0).astype(jnp.bfloat16)

    def hide(part_of):
        for r in range(2):
            row = id_buf[part_of, r : r + 1, :].astype(jnp.float32)
            column = jnp.broadcast_to(row, (WIDTH, WIDTH)).T
            at = part_of * SHARD + r * WIDTH
            key_pos = lax.broadcasted_iota(jnp.int32, (WIDTH, WIDTH), 0) + at
            query_pos = lax.broadcasted_iota(jnp.int32, (WIDTH, WIDTH), 1) + own
            for half in range(2):
                query = id_buf[BACK, half : half + 1, :].astype(jnp.float32)
                seen = column == query
                if part_of == BACK:
                    seen = seen & (key_pos <= query_pos + half * WIDTH)
                bias[half, pl.ds(at, WIDTH), :] = jnp.where(seen, 0.0, HIDE).astype(jnp.bfloat16)

    loads[0].wait()
    hide(BACK)
    for by in range(1, BACK + 1):

        @pl.when(ctx >= by)
        def _():
            move(0, BACK - by, ctx, False).wait_recv()

        hide(BACK - by)
    for load in loads[1:]:
        load.wait()
    for by in range(1, BACK + 1):

        @pl.when(ctx >= by)
        def _():
            move(1, BACK - by, ctx, False).wait_recv()
            move(2, BACK - by, ctx, False).wait_recv()

    def outgoing(step, piece):
        rows = pl.ds(pl.multiple_of(piece * TILE, TILE), TILE)
        slot = core * (1 - step // 2) + 2 * (step // 2)
        return pltpu.make_async_remote_copy(
            src_ref=stage.at[step, rows],
            dst_ref=out_hbm.at[rows, pl.ds(pl.multiple_of(kvh * GROUP * WIDTH, WIDTH), GROUP * WIDTH)],
            send_sem=out_send.at[step, piece], recv_sem=out_recv.at[slot, piece],
            device_id=(ctx, owner(step)), device_id_type=MESH,
        )

    def kept(piece):
        rows = pl.ds(pl.multiple_of(piece * TILE, TILE), TILE)
        return pltpu.make_async_copy(
            stage.at[3, rows],
            out_hbm.at[rows, pl.ds(pl.multiple_of(kvh * GROUP * WIDTH, WIDTH), GROUP * WIDTH)],
            own_sem.at[piece],
        )

    def work(i, _):
        step, piece = i // PIECES, i % PIECES
        block = owner(step)
        window = pl.ds(pl.multiple_of(block * BLOCK, BLOCK), WINDOW)
        keys = jnp.concatenate([k_buf[window, :], bias[block // 2, window, :]], axis=1)
        ones = jnp.ones((16, WINDOW), jnp.bfloat16)
        values = jnp.concatenate([v_buf[window, :].T, ones], axis=0)
        first = pl.multiple_of((block * PIECES + piece) * ROWS, ROWS)
        inside = pl.multiple_of(((block % 2) * PIECES + piece) * ROWS, ROWS)
        queries = jnp.concatenate([q_buf[pl.ds(first, ROWS), :], pick[pl.ds(inside, ROWS), :]], axis=1)
        score = lax.dot_general(keys, queries, LAST, preferred_element_type=jnp.float32)
        top = jnp.max(score, axis=0, keepdims=True)
        weight = jnp.exp2((score - top) * EXP2).astype(jnp.bfloat16)
        summed = lax.dot_general(values, weight, PLAIN, preferred_element_type=jnp.float32)
        turned[...] = (summed[:WIDTH] / summed[WIDTH : WIDTH + 1]).T
        tokens = pl.ds(pl.multiple_of(piece * TILE, TILE), TILE)
        for head in range(GROUP):
            stage[step, tokens, head * WIDTH : (head + 1) * WIDTH] = turned[
                pl.ds(head, TILE, stride=GROUP), :
            ].astype(jnp.bfloat16)

        @pl.when(step < 3)
        def _():
            outgoing(step, piece).start()

        @pl.when(step == 3)
        def _():
            kept(piece).start()

        return 0

    lax.fori_loop(0, 4 * PIECES, work, 0)

    for i in range(3):
        for by in range(1, BACK + 1):

            @pl.when(straight[by])
            def _():
                move(i, BACK - by, ctx, False).wait_send()

            @pl.when(onward[by])
            def _():
                move(i, BACK - by, ctx, True).wait_send()

        @pl.when(gives)
        def _():
            move(i, BACK + 1, ctx, False).wait_send()

    for piece in range(PIECES):
        kept(piece).wait()
        for step in range(3):
            outgoing(step, piece).wait_send()
        for slot in range(3):
            rows = pl.ds(piece * TILE, TILE)
            pltpu.make_async_remote_copy(
                src_ref=stage.at[slot, rows], dst_ref=out_hbm.at[rows, pl.ds(0, GROUP * WIDTH)],
                send_sem=out_send.at[slot, piece], recv_sem=out_recv.at[slot, piece],
                device_id=(ctx, owner(0)), device_id_type=MESH,
            ).wait_recv()


def body(queries, keys, values, doc_ids):
    anywhere = pl.BlockSpec(memory_space=pl.ANY)
    return pl.pallas_call(
        kernel,
        name="attend",
        out_shape=pltpu.VMEM((BLOCK, 4 * GROUP * WIDTH), jnp.bfloat16),
        in_specs=[anywhere] * 4,
        out_specs=pl.BlockSpec(memory_space=pltpu.VMEM),
        scratch_shapes=[
            pltpu.VMEM((SHARD * GROUP, WIDTH), jnp.bfloat16),
            pltpu.VMEM((KEYS, WIDTH), jnp.bfloat16),
            pltpu.VMEM((KEYS, WIDTH), jnp.bfloat16),
            pltpu.VMEM((BACK + 1, 2, WIDTH), jnp.int32),
            pltpu.VMEM((SHARD, WIDTH), jnp.bfloat16),
            pltpu.VMEM((SHARD, WIDTH), jnp.bfloat16),
            pltpu.VMEM((2, WIDTH), jnp.int32),
            pltpu.VMEM((SHARD // 2 * GROUP, WIDTH), jnp.bfloat16),
            pltpu.VMEM((2, KEYS, WIDTH), jnp.bfloat16),
            pltpu.VMEM((4, BLOCK, GROUP * WIDTH), jnp.bfloat16),
            pltpu.VMEM((ROWS, WIDTH), jnp.float32),
            pltpu.SemaphoreType.DMA((4,)),
            pltpu.SemaphoreType.DMA((2 * BACK + 1, 3)),
            pltpu.SemaphoreType.DMA((BACK + 1, 3)),
            pltpu.SemaphoreType.DMA((3, PIECES)),
            pltpu.SemaphoreType.DMA((3, PIECES)),
            pltpu.SemaphoreType.DMA((PIECES,)),
        ],
        compiler_params=pltpu.CompilerParams(
            collective_id=0, has_side_effects=True, vmem_limit_bytes=56 << 20
        ),
        cost_estimate=pl.CostEstimate(
            flops=4 * SHARD * GROUP * KEYS * WIDTH, bytes_accessed=4 << 20, transcendentals=SHARD * GROUP * KEYS
        ),
    )(
        queries.reshape(SHARD * GROUP, WIDTH),
        keys.reshape(SHARD, WIDTH),
        values.reshape(SHARD, WIDTH),
        doc_ids.reshape(2, WIDTH),
    )


def solution(mesh):
    return jax.shard_map(
        body,
        mesh=mesh,
        in_specs=(P("ctx", "kvh", None), P("ctx", "kvh", None), P("ctx", "kvh", None), P("ctx")),
        out_specs=P(("ctx", "kvh"), None),
        check_vma=False,
    )
```

```python
import functools

import jax
import jax.numpy as jnp
from jax import lax
from jax.experimental import pallas as pl
from jax.experimental.pallas import tpu as pltpu
from jax.sharding import PartitionSpec as P

MESH = pl.DeviceIdType.MESH
BACK = 3
RING = 4
CROSS = [(y, by) for y in range(RING) for by in range(1, BACK + 1) if y + by >= RING]
DIRECT = ([(1, 3), (2, 2), (2, 3), (3, 1)], [(1, 3), (2, 2), (2, 3), (3, 1)])
PASSED = [[flow for flow in CROSS if flow not in straight] for straight in DIRECT]
SHARD = 256
CUTS = 1
CUT = SHARD // CUTS
ITEMS = 1 + 2 * CUTS
GROUP = 16
WIDTH = 128
KEYS = (BACK + 1) * SHARD
BLOCK = 64
WINDOW = BACK * SHARD + 2 * BLOCK
TILE = 32
PIECES = BLOCK // TILE
ROWS = TILE * GROUP
HIDE = -131072.0
EXP2 = 1.4426950408889634 / WIDTH**0.5
LAST = (((1,), (1,)), ((), ()))
PLAIN = (((1,), (0,)), ((), ()))


def kernel(
    q_hbm, k_hbm, v_hbm, ids_hbm, out_hbm,
    q_buf, k_buf, v_buf, id_buf, vt_buf, k_pass, v_pass, id_pass, pick, bias, stage, turned,
    load_sem, kv_send, kv_recv, out_send, out_recv, own_sem,
):
    ctx = lax.axis_index("ctx")
    kvh = lax.axis_index("kvh")
    shards = lax.axis_size("ctx")
    pair, core = kvh // 2, kvh % 2

    ring, place = ctx // RING, ctx % RING
    rings = shards // RING

    def any_of(conditions):
        return functools.reduce(jnp.logical_or, conditions, False)

    def sends(flows, by=None):
        found = [(ring % 2 == i) & (place == y) for i in range(2) for y in sorted({y for y, b in flows[i] if by in (None, b)})]
        return (ring < rings - 1) & any_of(found)

    def after(flows, by=None, end=False):
        found = [
            (ring % 2 == 1 - i) & (place == y)
            for i in range(2)
            for y in sorted({y + (b - RING) * end for y, b in flows[i] if by in (None, b)})
        ]
        return (ring >= 1) & any_of(found)

    steps = range(1, BACK + 1)
    gives, takes = sends(PASSED), after(PASSED)
    straight = {by: (place + by < RING) | sends(DIRECT, by) for by in steps}
    reached = {by: (place >= by) | after(DIRECT, by, end=True) for by in steps}
    onward = {by: after(PASSED, by) for by in steps}
    fed = {by: after(PASSED, by, end=True) for by in steps}

    def owner(step):
        late, odd = step // 2, step % 2
        x = (1 - pair) * (1 - late) + pair * late
        c = (1 - odd) * (1 - late) + late * ((1 - core) * (1 - odd) + core * odd)
        return 2 * x + c

    barrier = pltpu.get_barrier_semaphore()
    for by in range(1, BACK + 1):

        @pl.when(reached[by])
        def _():
            pl.semaphore_signal(barrier, inc=1, device_id=(ctx - by, kvh), device_id_type=MESH)

        @pl.when(fed[by])
        def _():
            pl.semaphore_signal(barrier, inc=1, device_id=(ctx - by + RING, kvh), device_id_type=MESH)

    for step in range(3):
        pl.semaphore_signal(barrier, inc=1, device_id=(ctx, owner(step)), device_id_type=MESH)

    @pl.when(takes)
    def _():
        pl.semaphore_signal(barrier, inc=1, device_id=(ctx - RING, kvh), device_id_type=MESH)

    own = BACK * SHARD
    loads = [
        pltpu.make_async_copy(ids_hbm, id_buf.at[BACK], load_sem.at[0]),
        pltpu.make_async_copy(k_hbm, k_buf.at[pl.ds(own, SHARD)], load_sem.at[1]),
        pltpu.make_async_copy(v_hbm, v_buf.at[pl.ds(own, SHARD)], load_sem.at[2]),
        pltpu.make_async_copy(q_hbm, q_buf, load_sem.at[3]),
    ]
    for load in loads:
        load.start()

    sent_to = [gives, *straight.values(), *onward.values()]
    pl.semaphore_wait(barrier, 3 + sum(to.astype(jnp.int32) for to in sent_to))

    def part_rows(to, first=0, count=SHARD):
        return pl.ds(pl.multiple_of(to * SHARD + first, WIDTH), count)

    def part(i, to):
        if isinstance(to, int) and to == BACK + 1:
            return id_pass if i == 0 else (k_pass, v_pass)[(i - 1) // CUTS].at[pl.ds((i - 1) % CUTS * CUT, CUT)]
        if i == 0:
            return id_buf.at[to]
        return (k_buf, v_buf)[(i - 1) // CUTS].at[part_rows(to, (i - 1) % CUTS * CUT, CUT)]

    def move(i, to, target, passed):
        src = ids_hbm if i == 0 else (k_hbm, v_hbm)[(i - 1) // CUTS].at[pl.ds((i - 1) % CUTS * CUT, CUT)]
        slot = BACK if isinstance(to, int) and to > BACK else to
        if passed:
            src = part(i, BACK + 1)
        return pltpu.make_async_remote_copy(
            src_ref=src, dst_ref=part(i, to),
            send_sem=kv_send.at[slot + (BACK + 1) * passed, i], recv_sem=kv_recv.at[slot, i],
            device_id=(target, kvh), device_id_type=MESH,
        )

    @pl.when(gives)
    def _():
        for i in range(ITEMS):
            move(i, BACK + 1, ctx + RING, False).start()

    @pl.when(straight[1])
    def _():
        for i in range(ITEMS):
            move(i, BACK - 1, ctx + 1, False).start()

    for i in range(ITEMS):
        for by in (2, 3):

            @pl.when(straight[by])
            def _():
                move(i, BACK - by, ctx + by, False).start()

    for by in range(1, BACK + 1):

        @pl.when(ctx < by)
        def _():
            rows = pl.ds((BACK - by) * SHARD, SHARD)
            id_buf[BACK - by] = jnp.full((2, WIDTH), -1, jnp.int32)
            k_buf[rows] = jnp.zeros((SHARD, WIDTH), jnp.bfloat16)
            v_buf[rows] = jnp.zeros((SHARD, WIDTH), jnp.bfloat16)

    token = lax.broadcasted_iota(jnp.int32, (SHARD // 2 * GROUP, WIDTH), 0) // GROUP
    lane = lax.broadcasted_iota(jnp.int32, (SHARD // 2 * GROUP, WIDTH), 1)
    pick[...] = jnp.where(token == lane, 1.0, 0.0).astype(jnp.bfloat16)

    def hide(to, causal=False):
        for r in range(2):
            row = id_buf[to, r : r + 1, :].astype(jnp.float32)
            column = jnp.broadcast_to(row, (WIDTH, WIDTH)).T
            key_pos = lax.broadcasted_iota(jnp.int32, (WIDTH, WIDTH), 0) + r * WIDTH
            query_pos = lax.broadcasted_iota(jnp.int32, (WIDTH, WIDTH), 1)
            for half in range(2):
                query = id_buf[BACK, half : half + 1, :].astype(jnp.float32)
                seen = column == query
                if causal:
                    seen = seen & (key_pos <= query_pos + half * WIDTH)
                rows = part_rows(to, r * WIDTH, WIDTH)
                bias[half, rows, :] = jnp.where(seen, 0.0, HIDE).astype(jnp.bfloat16)

    def turn(to):
        vt_buf[:WIDTH, part_rows(to)] = v_buf[part_rows(to), :].T

    def arrived(to, items):
        @pl.when(ctx >= BACK - to)
        def _():
            for i in items:
                move(i, to, ctx, False).wait_recv()

    vt_buf[WIDTH:, :] = jnp.ones((16, KEYS), jnp.bfloat16)
    for load in loads:
        load.wait()
    hide(BACK, causal=True)
    turn(BACK)

    @pl.when(takes)
    def _():
        for i in range(ITEMS):
            move(i, BACK + 1, ctx, False).wait_recv()
            for by in range(1, BACK + 1):

                @pl.when(onward[by])
                def _():
                    move(i, BACK - by, ctx + by - RING, True).start()

    def outgoing(step, piece):
        rows = pl.ds(pl.multiple_of(piece * TILE, TILE), TILE)
        slot = core * (1 - step // 2) + 2 * (step // 2)
        return pltpu.make_async_remote_copy(
            src_ref=stage.at[step, rows],
            dst_ref=out_hbm.at[rows, pl.ds(pl.multiple_of(kvh * GROUP * WIDTH, WIDTH), GROUP * WIDTH)],
            send_sem=out_send.at[step, piece], recv_sem=out_recv.at[slot, piece],
            device_id=(ctx, owner(step)), device_id_type=MESH,
        )

    def kept(piece):
        rows = pl.ds(pl.multiple_of(piece * TILE, TILE), TILE)
        return pltpu.make_async_copy(
            stage.at[3, rows],
            out_hbm.at[rows, pl.ds(pl.multiple_of(kvh * GROUP * WIDTH, WIDTH), GROUP * WIDTH)],
            own_sem.at[piece],
        )

    def asked(step, piece):
        block = owner(step)
        first = pl.multiple_of((block * PIECES + piece) * ROWS, ROWS)
        inside = pl.multiple_of(((block % 2) * PIECES + piece) * ROWS, ROWS)
        return jnp.concatenate([q_buf[pl.ds(first, ROWS), :], pick[pl.ds(inside, ROWS), :]], axis=1)

    def scores(keys, queries):
        return lax.dot_general(keys, queries, LAST, preferred_element_type=jnp.float32)

    def weighed(values, score, top):
        weight = jnp.exp2((score - top) * EXP2).astype(jnp.bfloat16)
        return lax.dot_general(values, weight, PLAIN, preferred_element_type=jnp.float32)

    def finish(step, piece, summed):
        turned[...] = (summed[:WIDTH] / summed[WIDTH : WIDTH + 1]).T
        tokens = pl.ds(pl.multiple_of(piece * TILE, TILE), TILE)
        for head in range(GROUP):
            stage[step, tokens, head * WIDTH : (head + 1) * WIDTH] = turned[
                pl.ds(head, TILE, stride=GROUP), :
            ].astype(jnp.bfloat16)

    late = (BACK - 1 - place) * (1 - place // BACK)
    early = [1 - (late + 1) // 2, 2 - late // 2, BACK]
    for to in early[:2]:
        arrived(to, range(ITEMS))
        hide(to)
        turn(to)
    half = owner(0) // 2
    queries = asked(0, 0)

    def keys_of(to):
        return jnp.concatenate([k_buf[part_rows(to), :], bias[half, part_rows(to), :]], axis=1)

    score = scores(jnp.concatenate([keys_of(to) for to in early], axis=0), queries)
    early_top = jnp.max(score, axis=0, keepdims=True)
    early_sum = weighed(jnp.concatenate([vt_buf[:, part_rows(to)] for to in early], axis=1), score, early_top)
    arrived(late, [0])
    hide(late)
    arrived(late, range(1, ITEMS))
    turn(late)
    score = scores(keys_of(late), queries)
    top = jnp.maximum(early_top, jnp.max(score, axis=0, keepdims=True))
    late_sum = weighed(vt_buf[:, part_rows(late)], score, top)
    finish(0, 0, early_sum * jnp.exp2((early_top - top) * EXP2) + late_sum)
    outgoing(0, 0).start()

    def work(i, _):
        step, piece = i // PIECES, i % PIECES
        block = owner(step)
        window = pl.ds(pl.multiple_of(block // 2 * WIDTH, WIDTH), WINDOW)
        score = scores(jnp.concatenate([k_buf[window, :], bias[block // 2, window, :]], axis=1), asked(step, piece))
        top = jnp.max(score, axis=0, keepdims=True)
        finish(step, piece, weighed(vt_buf[:, window], score, top))

        @pl.when(step < 3)
        def _():
            outgoing(step, piece).start()

        @pl.when(step == 3)
        def _():
            kept(piece).start()

        return 0

    lax.fori_loop(1, 4 * PIECES, work, 0)

    for i in range(ITEMS):
        for by in range(1, BACK + 1):

            @pl.when(straight[by])
            def _():
                move(i, BACK - by, ctx, False).wait_send()

            @pl.when(onward[by])
            def _():
                move(i, BACK - by, ctx, True).wait_send()

        @pl.when(gives)
        def _():
            move(i, BACK + 1, ctx, False).wait_send()

    for piece in range(PIECES):
        kept(piece).wait()
        for step in range(3):
            outgoing(step, piece).wait_send()
        for slot in range(3):
            rows = pl.ds(piece * TILE, TILE)
            pltpu.make_async_remote_copy(
                src_ref=stage.at[slot, rows], dst_ref=out_hbm.at[rows, pl.ds(0, GROUP * WIDTH)],
                send_sem=out_send.at[slot, piece], recv_sem=out_recv.at[slot, piece],
                device_id=(ctx, owner(0)), device_id_type=MESH,
            ).wait_recv()


def body(queries, keys, values, doc_ids):
    anywhere = pl.BlockSpec(memory_space=pl.ANY)
    return pl.pallas_call(
        kernel,
        name="attend",
        out_shape=pltpu.VMEM((BLOCK, 4 * GROUP * WIDTH), jnp.bfloat16),
        in_specs=[anywhere] * 4,
        out_specs=pl.BlockSpec(memory_space=pltpu.VMEM),
        scratch_shapes=[
            pltpu.VMEM((SHARD * GROUP, WIDTH), jnp.bfloat16),
            pltpu.VMEM((KEYS, WIDTH), jnp.bfloat16),
            pltpu.VMEM((KEYS, WIDTH), jnp.bfloat16),
            pltpu.VMEM((BACK + 1, 2, WIDTH), jnp.int32),
            pltpu.VMEM((WIDTH + 16, KEYS), jnp.bfloat16),
            pltpu.VMEM((SHARD, WIDTH), jnp.bfloat16),
            pltpu.VMEM((SHARD, WIDTH), jnp.bfloat16),
            pltpu.VMEM((2, WIDTH), jnp.int32),
            pltpu.VMEM((SHARD // 2 * GROUP, WIDTH), jnp.bfloat16),
            pltpu.VMEM((2, KEYS, WIDTH), jnp.bfloat16),
            pltpu.VMEM((4, BLOCK, GROUP * WIDTH), jnp.bfloat16),
            pltpu.VMEM((ROWS, WIDTH), jnp.float32),
            pltpu.SemaphoreType.DMA((4,)),
            pltpu.SemaphoreType.DMA((2 * BACK + 1, ITEMS)),
            pltpu.SemaphoreType.DMA((BACK + 1, ITEMS)),
            pltpu.SemaphoreType.DMA((3, PIECES)),
            pltpu.SemaphoreType.DMA((3, PIECES)),
            pltpu.SemaphoreType.DMA((PIECES,)),
        ],
        compiler_params=pltpu.CompilerParams(
            collective_id=0, has_side_effects=True, vmem_limit_bytes=56 << 20
        ),
        cost_estimate=pl.CostEstimate(
            flops=4 * SHARD * GROUP * KEYS * WIDTH, bytes_accessed=4 << 20, transcendentals=SHARD * GROUP * KEYS
        ),
    )(
        queries.reshape(SHARD * GROUP, WIDTH),
        keys.reshape(SHARD, WIDTH),
        values.reshape(SHARD, WIDTH),
        doc_ids.reshape(2, WIDTH),
    )


def solution(mesh):
    return jax.shard_map(
        body,
        mesh=mesh,
        in_specs=(P("ctx", "kvh", None), P("ctx", "kvh", None), P("ctx", "kvh", None), P("ctx")),
        out_specs=P(("ctx", "kvh"), None),
        check_vma=False,
    )
```

```python
import functools

import jax
import jax.numpy as jnp
from jax import lax
from jax.experimental import pallas as pl
from jax.experimental.pallas import tpu as pltpu
from jax.sharding import PartitionSpec as P

MESH = pl.DeviceIdType.MESH
BACK = 3
RING = 4
CROSS = [(y, by) for y in range(RING) for by in range(1, BACK + 1) if y + by >= RING]
DIRECT = ([(1, 3), (2, 2), (2, 3), (3, 1)], [(1, 3), (2, 2), (2, 3), (3, 1)])
PASSED = [[flow for flow in CROSS if flow not in straight] for straight in DIRECT]
SHARD = 256
LANDED = SHARD + 16
ITEMS = 2
GROUP = 16
WIDTH = 128
KEYS = (BACK + 1) * SHARD
BLOCK = 64
WINDOW = BACK * SHARD + 2 * BLOCK
TILE = 32
PIECES = BLOCK // TILE
ROWS = TILE * GROUP
HIDE = -131072.0
EXP2 = 1.4426950408889634 / WIDTH**0.5
LAST = (((1,), (1,)), ((), ()))
PLAIN = (((1,), (0,)), ((), ()))


def kernel(
    q_hbm, k_hbm, v_hbm, ids_hbm, out_hbm,
    q_buf, k_buf, v_buf, own_ids, vt_buf, k_pass, v_pass, pick, bias, stage, turned,
    load_sem, kv_send, kv_recv, out_send, out_recv, own_sem,
):
    ctx = lax.axis_index("ctx")
    kvh = lax.axis_index("kvh")
    shards = lax.axis_size("ctx")
    pair, core = kvh // 2, kvh % 2

    ring, place = ctx // RING, ctx % RING
    rings = shards // RING

    def any_of(conditions):
        return functools.reduce(jnp.logical_or, conditions, False)

    def sends(flows, by=None):
        found = [(ring % 2 == i) & (place == y) for i in range(2) for y in sorted({y for y, b in flows[i] if by in (None, b)})]
        return (ring < rings - 1) & any_of(found)

    def after(flows, by=None, end=False):
        found = [
            (ring % 2 == 1 - i) & (place == y)
            for i in range(2)
            for y in sorted({y + (b - RING) * end for y, b in flows[i] if by in (None, b)})
        ]
        return (ring >= 1) & any_of(found)

    steps = range(1, BACK + 1)
    gives, takes = sends(PASSED), after(PASSED)
    straight = {by: (place + by < RING) | sends(DIRECT, by) for by in steps}
    reached = {by: (place >= by) | after(DIRECT, by, end=True) for by in steps}
    onward = {by: after(PASSED, by) for by in steps}
    fed = {by: after(PASSED, by, end=True) for by in steps}

    def owner(step):
        late, odd = step // 2, step % 2
        x = (1 - pair) * (1 - late) + pair * late
        c = (1 - odd) * (1 - late) + late * ((1 - core) * (1 - odd) + core * odd)
        return 2 * x + c

    barrier = pltpu.get_barrier_semaphore()
    for step in range(3):
        pl.semaphore_signal(barrier, inc=1, device_id=(ctx, owner(step)), device_id_type=MESH)

    for by in range(1, BACK + 1):

        @pl.when(reached[by])
        def _():
            pl.semaphore_signal(barrier, inc=1, device_id=(ctx - by, kvh), device_id_type=MESH)

        @pl.when(fed[by])
        def _():
            pl.semaphore_signal(barrier, inc=1, device_id=(ctx - by + RING, kvh), device_id_type=MESH)

    @pl.when(takes)
    def _():
        pl.semaphore_signal(barrier, inc=1, device_id=(ctx - RING, kvh), device_id_type=MESH)

    own = BACK * SHARD
    loads = [
        pltpu.make_async_copy(ids_hbm, own_ids, load_sem.at[0]),
        pltpu.make_async_copy(k_hbm, k_buf.at[pl.ds(own, SHARD)], load_sem.at[1]),
        pltpu.make_async_copy(v_hbm, v_buf.at[BACK, pl.ds(0, SHARD)], load_sem.at[2]),
        pltpu.make_async_copy(q_hbm, q_buf, load_sem.at[3]),
    ]
    for load in loads:
        load.start()

    for load in loads[:3]:
        load.wait()
    ids = jnp.concatenate([own_ids[...].astype(jnp.float32), jnp.zeros((14, WIDTH), jnp.float32)], axis=0)
    v_buf[BACK, SHARD:, :] = ids.astype(jnp.bfloat16)

    sent_to = [gives, *straight.values(), *onward.values()]
    pl.semaphore_wait(barrier, 3 + sum(to.astype(jnp.int32) for to in sent_to))

    def part_rows(to, first=0, count=SHARD):
        return pl.ds(pl.multiple_of(to * SHARD + first, WIDTH), count)

    def part(i, to):
        if isinstance(to, int) and to == BACK + 1:
            return (v_pass, k_pass)[i]
        return v_buf.at[to] if i == 0 else k_buf.at[part_rows(to)]

    def move(i, to, target, passed):
        src = part(i, BACK)
        slot = BACK if isinstance(to, int) and to > BACK else to
        if passed:
            src = part(i, BACK + 1)
        return pltpu.make_async_remote_copy(
            src_ref=src, dst_ref=part(i, to),
            send_sem=kv_send.at[slot + (BACK + 1) * passed, i], recv_sem=kv_recv.at[slot, i],
            device_id=(target, kvh), device_id_type=MESH,
        )

    @pl.when(gives)
    def _():
        for i in range(ITEMS):
            move(i, BACK + 1, ctx + RING, False).start()

    @pl.when(straight[1])
    def _():
        for i in range(ITEMS):
            move(i, BACK - 1, ctx + 1, False).start()

    for i in range(ITEMS):
        for by in (2, 3):

            @pl.when(straight[by])
            def _():
                move(i, BACK - by, ctx + by, False).start()

    for by in range(1, BACK + 1):

        @pl.when(ctx < by)
        def _():
            rows = pl.ds((BACK - by) * SHARD, SHARD)
            k_buf[rows] = jnp.zeros((SHARD, WIDTH), jnp.bfloat16)
            v_buf[BACK - by, :SHARD, :] = jnp.zeros((SHARD, WIDTH), jnp.bfloat16)
            v_buf[BACK - by, SHARD:, :] = jnp.full((16, WIDTH), -1, jnp.bfloat16)

    token = lax.broadcasted_iota(jnp.int32, (SHARD // 2 * GROUP, WIDTH), 0) // GROUP
    lane = lax.broadcasted_iota(jnp.int32, (SHARD // 2 * GROUP, WIDTH), 1)
    pick[...] = jnp.where(token == lane, 1.0, 0.0).astype(jnp.bfloat16)

    def hide(to, causal=False):
        key_ids = v_buf[to, SHARD:, :].astype(jnp.float32)
        query_ids = v_buf[BACK, SHARD:, :].astype(jnp.float32)
        for r in range(2):
            column = jnp.broadcast_to(key_ids[r : r + 1], (WIDTH, WIDTH)).T
            key_pos = lax.broadcasted_iota(jnp.int32, (WIDTH, WIDTH), 0) + r * WIDTH
            query_pos = lax.broadcasted_iota(jnp.int32, (WIDTH, WIDTH), 1)
            for half in range(2):
                seen = column == query_ids[half : half + 1]
                if causal:
                    seen = seen & (key_pos <= query_pos + half * WIDTH)
                rows = part_rows(to, r * WIDTH, WIDTH)
                bias[half, rows, :] = jnp.where(seen, 0.0, HIDE).astype(jnp.bfloat16)

    def turn(to):
        vt_buf[:WIDTH, part_rows(to)] = v_buf[to, :SHARD, :].T

    def arrived(to, items):
        @pl.when(ctx >= BACK - to)
        def _():
            for i in items:
                move(i, to, ctx, False).wait_recv()

    vt_buf[WIDTH:, :] = jnp.ones((16, KEYS), jnp.bfloat16)
    loads[3].wait()
    hide(BACK, causal=True)
    turn(BACK)

    @pl.when(takes)
    def _():
        for i in range(ITEMS):
            move(i, BACK + 1, ctx, False).wait_recv()
            for by in range(1, BACK + 1):

                @pl.when(onward[by])
                def _():
                    move(i, BACK - by, ctx + by - RING, True).start()

    def outgoing(step, piece):
        rows = pl.ds(pl.multiple_of(piece * TILE, TILE), TILE)
        slot = core * (1 - step // 2) + 2 * (step // 2)
        return pltpu.make_async_remote_copy(
            src_ref=stage.at[step, rows],
            dst_ref=out_hbm.at[rows, pl.ds(pl.multiple_of(kvh * GROUP * WIDTH, WIDTH), GROUP * WIDTH)],
            send_sem=out_send.at[step, piece], recv_sem=out_recv.at[slot, piece],
            device_id=(ctx, owner(step)), device_id_type=MESH,
        )

    def kept(piece):
        rows = pl.ds(pl.multiple_of(piece * TILE, TILE), TILE)
        return pltpu.make_async_copy(
            stage.at[3, rows],
            out_hbm.at[rows, pl.ds(pl.multiple_of(kvh * GROUP * WIDTH, WIDTH), GROUP * WIDTH)],
            own_sem.at[piece],
        )

    def asked(step, piece):
        block = owner(step)
        first = pl.multiple_of((block * PIECES + piece) * ROWS, ROWS)
        inside = pl.multiple_of(((block % 2) * PIECES + piece) * ROWS, ROWS)
        return jnp.concatenate([q_buf[pl.ds(first, ROWS), :], pick[pl.ds(inside, ROWS), :]], axis=1)

    def scores(keys, queries):
        return lax.dot_general(keys, queries, LAST, preferred_element_type=jnp.float32)

    def weighed(values, score, top):
        weight = jnp.exp2((score - top) * EXP2).astype(jnp.bfloat16)
        return lax.dot_general(values, weight, PLAIN, preferred_element_type=jnp.float32)

    def finish(step, piece, summed):
        turned[...] = (summed[:WIDTH] / summed[WIDTH : WIDTH + 1]).T
        tokens = pl.ds(pl.multiple_of(piece * TILE, TILE), TILE)
        for head in range(GROUP):
            stage[step, tokens, head * WIDTH : (head + 1) * WIDTH] = turned[
                pl.ds(head, TILE, stride=GROUP), :
            ].astype(jnp.bfloat16)

    late = (BACK - 1 - place) * (1 - place // BACK)
    early = [1 - (late + 1) // 2, 2 - late // 2, BACK]
    for to in early[:2]:
        arrived(to, range(ITEMS))
        hide(to)
        turn(to)
    half = owner(0) // 2
    queries = asked(0, 0)

    def keys_of(to):
        return jnp.concatenate([k_buf[part_rows(to), :], bias[half, part_rows(to), :]], axis=1)

    score = scores(jnp.concatenate([keys_of(to) for to in early], axis=0), queries)
    early_top = jnp.max(score, axis=0, keepdims=True)
    early_sum = weighed(jnp.concatenate([vt_buf[:, part_rows(to)] for to in early], axis=1), score, early_top)
    arrived(late, [0])
    hide(late)
    turn(late)
    arrived(late, [1])
    score = scores(keys_of(late), queries)
    top = jnp.maximum(early_top, jnp.max(score, axis=0, keepdims=True))
    late_sum = weighed(vt_buf[:, part_rows(late)], score, top)
    finish(0, 0, early_sum * jnp.exp2((early_top - top) * EXP2) + late_sum)
    outgoing(0, 0).start()

    def work(i, _):
        step, piece = i // PIECES, i % PIECES
        block = owner(step)
        window = pl.ds(pl.multiple_of(block // 2 * WIDTH, WIDTH), WINDOW)
        score = scores(jnp.concatenate([k_buf[window, :], bias[block // 2, window, :]], axis=1), asked(step, piece))
        top = jnp.max(score, axis=0, keepdims=True)
        finish(step, piece, weighed(vt_buf[:, window], score, top))

        @pl.when(step < 3)
        def _():
            outgoing(step, piece).start()

        @pl.when(step == 3)
        def _():
            kept(piece).start()

        return 0

    lax.fori_loop(1, 4 * PIECES, work, 0)

    for i in range(ITEMS):
        for by in range(1, BACK + 1):

            @pl.when(straight[by])
            def _():
                move(i, BACK - by, ctx, False).wait_send()

            @pl.when(onward[by])
            def _():
                move(i, BACK - by, ctx, True).wait_send()

        @pl.when(gives)
        def _():
            move(i, BACK + 1, ctx, False).wait_send()

    for piece in range(PIECES):
        kept(piece).wait()
        for step in range(3):
            outgoing(step, piece).wait_send()
        for slot in range(3):
            rows = pl.ds(piece * TILE, TILE)
            pltpu.make_async_remote_copy(
                src_ref=stage.at[slot, rows], dst_ref=out_hbm.at[rows, pl.ds(0, GROUP * WIDTH)],
                send_sem=out_send.at[slot, piece], recv_sem=out_recv.at[slot, piece],
                device_id=(ctx, owner(0)), device_id_type=MESH,
            ).wait_recv()


def body(queries, keys, values, doc_ids):
    anywhere = pl.BlockSpec(memory_space=pl.ANY)
    return pl.pallas_call(
        kernel,
        name="attend",
        out_shape=pltpu.VMEM((BLOCK, 4 * GROUP * WIDTH), jnp.bfloat16),
        in_specs=[anywhere] * 4,
        out_specs=pl.BlockSpec(memory_space=pltpu.VMEM),
        scratch_shapes=[
            pltpu.VMEM((SHARD * GROUP, WIDTH), jnp.bfloat16),
            pltpu.VMEM((KEYS, WIDTH), jnp.bfloat16),
            pltpu.VMEM((BACK + 1, LANDED, WIDTH), jnp.bfloat16),
            pltpu.VMEM((2, WIDTH), jnp.int32),
            pltpu.VMEM((WIDTH + 16, KEYS), jnp.bfloat16),
            pltpu.VMEM((SHARD, WIDTH), jnp.bfloat16),
            pltpu.VMEM((LANDED, WIDTH), jnp.bfloat16),
            pltpu.VMEM((SHARD // 2 * GROUP, WIDTH), jnp.bfloat16),
            pltpu.VMEM((2, KEYS, WIDTH), jnp.bfloat16),
            pltpu.VMEM((4, BLOCK, GROUP * WIDTH), jnp.bfloat16),
            pltpu.VMEM((ROWS, WIDTH), jnp.float32),
            pltpu.SemaphoreType.DMA((4,)),
            pltpu.SemaphoreType.DMA((2 * BACK + 1, ITEMS)),
            pltpu.SemaphoreType.DMA((BACK + 1, ITEMS)),
            pltpu.SemaphoreType.DMA((3, PIECES)),
            pltpu.SemaphoreType.DMA((3, PIECES)),
            pltpu.SemaphoreType.DMA((PIECES,)),
        ],
        compiler_params=pltpu.CompilerParams(
            collective_id=0, has_side_effects=True, vmem_limit_bytes=56 << 20
        ),
        cost_estimate=pl.CostEstimate(
            flops=4 * SHARD * GROUP * KEYS * WIDTH, bytes_accessed=4 << 20, transcendentals=SHARD * GROUP * KEYS
        ),
    )(
        queries.reshape(SHARD * GROUP, WIDTH),
        keys.reshape(SHARD, WIDTH),
        values.reshape(SHARD, WIDTH),
        doc_ids.reshape(2, WIDTH),
    )


def solution(mesh):
    return jax.shard_map(
        body,
        mesh=mesh,
        in_specs=(P("ctx", "kvh", None), P("ctx", "kvh", None), P("ctx", "kvh", None), P("ctx")),
        out_specs=P(("ctx", "kvh"), None),
        check_vma=False,
    )
```

```python
import functools

import jax
import jax.numpy as jnp
from jax import lax
from jax.experimental import pallas as pl
from jax.experimental.pallas import tpu as pltpu
from jax.sharding import PartitionSpec as P

MESH = pl.DeviceIdType.MESH
BACK = 3
RING = 4
CROSS = [(y, by) for y in range(RING) for by in range(1, BACK + 1) if y + by >= RING]
DIRECT = ([(1, 3), (2, 2), (2, 3), (3, 1)], [(1, 3), (2, 2), (2, 3), (3, 1)])
PASSED = [[flow for flow in CROSS if flow not in straight] for straight in DIRECT]
SHARD = 256
LANDED = SHARD + 16
ITEMS = 2
GROUP = 16
WIDTH = 128
KEYS = (BACK + 1) * SHARD
BLOCK = 64
WINDOW = BACK * SHARD + 2 * BLOCK
TILE = 32
PIECES = BLOCK // TILE
ROWS = TILE * GROUP
HIDE = -131072.0
EXP2 = 1.4426950408889634 / WIDTH**0.5
LAST = (((1,), (1,)), ((), ()))
PLAIN = (((1,), (0,)), ((), ()))


def kernel(
    q_hbm, k_hbm, v_hbm, ids_hbm, out_hbm,
    q_buf, k_buf, v_buf, own_ids, vt_buf, k_pass, v_pass, pick, bias, stage, turned,
    load_sem, kv_send, kv_recv, out_send, out_recv, own_sem,
):
    ctx = lax.axis_index("ctx")
    kvh = lax.axis_index("kvh")
    shards = lax.axis_size("ctx")
    pair, core = kvh // 2, kvh % 2

    ring, place = ctx // RING, ctx % RING
    rings = shards // RING

    def any_of(conditions):
        return functools.reduce(jnp.logical_or, conditions, False)

    def sends(flows, by=None):
        found = [(ring % 2 == i) & (place == y) for i in range(2) for y in sorted({y for y, b in flows[i] if by in (None, b)})]
        return (ring < rings - 1) & any_of(found)

    def after(flows, by=None, end=False):
        found = [
            (ring % 2 == 1 - i) & (place == y)
            for i in range(2)
            for y in sorted({y + (b - RING) * end for y, b in flows[i] if by in (None, b)})
        ]
        return (ring >= 1) & any_of(found)

    steps = range(1, BACK + 1)
    gives, takes = sends(PASSED), after(PASSED)
    straight = {by: (place + by < RING) | sends(DIRECT, by) for by in steps}
    reached = {by: (place >= by) | after(DIRECT, by, end=True) for by in steps}
    onward = {by: after(PASSED, by) for by in steps}
    fed = {by: after(PASSED, by, end=True) for by in steps}

    def owner(step):
        late, odd = step // 2, step % 2
        x = (1 - pair) * (1 - late) + pair * late
        c = (1 - odd) * (1 - late) + late * ((1 - core) * (1 - odd) + core * odd)
        return 2 * x + c

    barrier = pltpu.get_barrier_semaphore()
    for step in range(3):
        pl.semaphore_signal(barrier, inc=1, device_id=(ctx, owner(step)), device_id_type=MESH)

    for by in range(1, BACK + 1):

        @pl.when(reached[by])
        def _():
            pl.semaphore_signal(barrier, inc=1, device_id=(ctx - by, kvh), device_id_type=MESH)

        @pl.when(fed[by])
        def _():
            pl.semaphore_signal(barrier, inc=1, device_id=(ctx - by + RING, kvh), device_id_type=MESH)

    @pl.when(takes)
    def _():
        pl.semaphore_signal(barrier, inc=1, device_id=(ctx - RING, kvh), device_id_type=MESH)

    own = BACK * SHARD
    loads = [
        pltpu.make_async_copy(ids_hbm, own_ids, load_sem.at[0]),
        pltpu.make_async_copy(k_hbm, k_buf.at[pl.ds(own, SHARD)], load_sem.at[1]),
        pltpu.make_async_copy(v_hbm, v_buf.at[BACK, pl.ds(0, SHARD)], load_sem.at[2]),
        pltpu.make_async_copy(q_hbm, q_buf, load_sem.at[3]),
    ]
    for load in loads:
        load.start()

    for load in loads[:3]:
        load.wait()
    ids = jnp.concatenate([own_ids[...].astype(jnp.float32), jnp.zeros((14, WIDTH), jnp.float32)], axis=0)
    v_buf[BACK, SHARD:, :] = ids.astype(jnp.bfloat16)

    sent_to = [gives, *straight.values(), *onward.values()]
    pl.semaphore_wait(barrier, 3 + sum(to.astype(jnp.int32) for to in sent_to))

    def part_rows(to, first=0, count=SHARD):
        return pl.ds(pl.multiple_of(to * SHARD + first, WIDTH), count)

    def part(i, to):
        if isinstance(to, int) and to == BACK + 1:
            return (v_pass, k_pass)[i]
        return v_buf.at[to] if i == 0 else k_buf.at[part_rows(to)]

    def move(i, to, target, passed):
        src = part(i, BACK)
        slot = BACK if isinstance(to, int) and to > BACK else to
        if passed:
            src = part(i, BACK + 1)
        return pltpu.make_async_remote_copy(
            src_ref=src, dst_ref=part(i, to),
            send_sem=kv_send.at[slot + (BACK + 1) * passed, i], recv_sem=kv_recv.at[slot, i],
            device_id=(target, kvh), device_id_type=MESH,
        )

    @pl.when(gives)
    def _():
        for i in range(ITEMS):
            move(i, BACK + 1, ctx + RING, False).start()

    @pl.when(straight[1])
    def _():
        for i in range(ITEMS):
            move(i, BACK - 1, ctx + 1, False).start()

    for i in range(ITEMS):
        for by in (2, 3):

            @pl.when(straight[by])
            def _():
                move(i, BACK - by, ctx + by, False).start()

    for by in range(1, BACK + 1):

        @pl.when(ctx < by)
        def _():
            rows = pl.ds((BACK - by) * SHARD, SHARD)
            k_buf[rows] = jnp.zeros((SHARD, WIDTH), jnp.bfloat16)
            v_buf[BACK - by, :SHARD, :] = jnp.zeros((SHARD, WIDTH), jnp.bfloat16)
            v_buf[BACK - by, SHARD:, :] = jnp.full((16, WIDTH), -1, jnp.bfloat16)

    token = lax.broadcasted_iota(jnp.int32, (SHARD // 2 * GROUP, WIDTH), 0) // GROUP
    lane = lax.broadcasted_iota(jnp.int32, (SHARD // 2 * GROUP, WIDTH), 1)
    pick[...] = jnp.where(token == lane, 1.0, 0.0).astype(jnp.bfloat16)

    def hide(to, causal=False):
        key_ids = v_buf[to, SHARD:, :].astype(jnp.float32)
        query_ids = v_buf[BACK, SHARD:, :].astype(jnp.float32)
        for r in range(2):
            column = jnp.broadcast_to(key_ids[r : r + 1], (WIDTH, WIDTH)).T
            key_pos = lax.broadcasted_iota(jnp.int32, (WIDTH, WIDTH), 0) + r * WIDTH
            query_pos = lax.broadcasted_iota(jnp.int32, (WIDTH, WIDTH), 1)
            for half in range(2):
                seen = column == query_ids[half : half + 1]
                if causal:
                    seen = seen & (key_pos <= query_pos + half * WIDTH)
                rows = part_rows(to, r * WIDTH, WIDTH)
                bias[half, rows, :] = jnp.where(seen, 0.0, HIDE).astype(jnp.bfloat16)

    def turn(to):
        vt_buf[:WIDTH, part_rows(to)] = v_buf[to, :SHARD, :].T

    def arrived(to, items):
        @pl.when(ctx >= BACK - to)
        def _():
            for i in items:
                move(i, to, ctx, False).wait_recv()

    vt_buf[WIDTH:, :] = jnp.ones((16, KEYS), jnp.bfloat16)
    loads[3].wait()
    hide(BACK, causal=True)
    turn(BACK)

    @pl.when(takes)
    def _():
        for i in range(ITEMS):
            move(i, BACK + 1, ctx, False).wait_recv()
            for by in range(1, BACK + 1):

                @pl.when(onward[by])
                def _():
                    move(i, BACK - by, ctx + by - RING, True).start()

    def outgoing(step, piece):
        rows = pl.ds(pl.multiple_of(piece * TILE, TILE), TILE)
        slot = core * (1 - step // 2) + 2 * (step // 2)
        return pltpu.make_async_remote_copy(
            src_ref=stage.at[step, rows],
            dst_ref=out_hbm.at[rows, pl.ds(pl.multiple_of(kvh * GROUP * WIDTH, WIDTH), GROUP * WIDTH)],
            send_sem=out_send.at[step, piece], recv_sem=out_recv.at[slot, piece],
            device_id=(ctx, owner(step)), device_id_type=MESH,
        )

    def kept(piece):
        rows = pl.ds(pl.multiple_of(piece * TILE, TILE), TILE)
        return pltpu.make_async_copy(
            stage.at[3, rows],
            out_hbm.at[rows, pl.ds(pl.multiple_of(kvh * GROUP * WIDTH, WIDTH), GROUP * WIDTH)],
            own_sem.at[piece],
        )

    def asked(step, piece):
        block = owner(step)
        first = pl.multiple_of((block * PIECES + piece) * ROWS, ROWS)
        inside = pl.multiple_of(((block % 2) * PIECES + piece) * ROWS, ROWS)
        return jnp.concatenate([q_buf[pl.ds(first, ROWS), :], pick[pl.ds(inside, ROWS), :]], axis=1)

    def scores(keys, queries):
        return lax.dot_general(keys, queries, LAST, preferred_element_type=jnp.float32)

    def weighed(values, score, top):
        weight = jnp.exp2((score - top) * EXP2).astype(jnp.bfloat16)
        return lax.dot_general(values, weight, PLAIN, preferred_element_type=jnp.float32)

    def finish(step, piece, summed):
        turned[...] = (summed[:WIDTH] * (1.0 / summed[WIDTH : WIDTH + 1])).T
        tokens = pl.ds(pl.multiple_of(piece * TILE, TILE), TILE)
        for head in range(GROUP):
            stage[step, tokens, head * WIDTH : (head + 1) * WIDTH] = turned[
                pl.ds(head, TILE, stride=GROUP), :
            ].astype(jnp.bfloat16)

    late = (BACK - 1 - place) * (1 - place // BACK)
    early = [1 - (late + 1) // 2, 2 - late // 2, BACK]
    for to in early[:2]:
        arrived(to, range(ITEMS))
        hide(to)
        turn(to)
    half = owner(0) // 2
    queries = asked(0, 0)

    def keys_of(to):
        return jnp.concatenate([k_buf[part_rows(to), :], bias[half, part_rows(to), :]], axis=1)

    score = scores(jnp.concatenate([keys_of(to) for to in early], axis=0), queries)
    early_top = jnp.max(score, axis=0, keepdims=True)
    early_sum = weighed(jnp.concatenate([vt_buf[:, part_rows(to)] for to in early], axis=1), score, early_top)
    arrived(late, [0])
    hide(late)
    turn(late)
    arrived(late, [1])
    score = scores(keys_of(late), queries)
    top = jnp.maximum(early_top, jnp.max(score, axis=0, keepdims=True))
    late_sum = weighed(vt_buf[:, part_rows(late)], score, top)
    finish(0, 0, early_sum * jnp.exp2((early_top - top) * EXP2) + late_sum)
    outgoing(0, 0).start()

    def work(i, _):
        step, piece = i // PIECES, i % PIECES
        block = owner(step)
        window = pl.ds(pl.multiple_of(block // 2 * WIDTH, WIDTH), WINDOW)
        score = scores(jnp.concatenate([k_buf[window, :], bias[block // 2, window, :]], axis=1), asked(step, piece))
        top = jnp.max(score, axis=0, keepdims=True)
        finish(step, piece, weighed(vt_buf[:, window], score, top))

        @pl.when(step < 3)
        def _():
            outgoing(step, piece).start()

        @pl.when(step == 3)
        def _():
            kept(piece).start()

        return 0

    lax.fori_loop(1, 4 * PIECES, work, 0)

    for i in range(ITEMS):
        for by in range(1, BACK + 1):

            @pl.when(straight[by])
            def _():
                move(i, BACK - by, ctx, False).wait_send()

            @pl.when(onward[by])
            def _():
                move(i, BACK - by, ctx, True).wait_send()

        @pl.when(gives)
        def _():
            move(i, BACK + 1, ctx, False).wait_send()

    for piece in range(PIECES):
        kept(piece).wait()
        for step in range(3):
            outgoing(step, piece).wait_send()
        for slot in range(3):
            rows = pl.ds(piece * TILE, TILE)
            pltpu.make_async_remote_copy(
                src_ref=stage.at[slot, rows], dst_ref=out_hbm.at[rows, pl.ds(0, GROUP * WIDTH)],
                send_sem=out_send.at[slot, piece], recv_sem=out_recv.at[slot, piece],
                device_id=(ctx, owner(0)), device_id_type=MESH,
            ).wait_recv()


def body(queries, keys, values, doc_ids):
    anywhere = pl.BlockSpec(memory_space=pl.ANY)
    return pl.pallas_call(
        kernel,
        name="attend",
        out_shape=pltpu.VMEM((BLOCK, 4 * GROUP * WIDTH), jnp.bfloat16),
        in_specs=[anywhere] * 4,
        out_specs=pl.BlockSpec(memory_space=pltpu.VMEM),
        scratch_shapes=[
            pltpu.VMEM((SHARD * GROUP, WIDTH), jnp.bfloat16),
            pltpu.VMEM((KEYS, WIDTH), jnp.bfloat16),
            pltpu.VMEM((BACK + 1, LANDED, WIDTH), jnp.bfloat16),
            pltpu.VMEM((2, WIDTH), jnp.int32),
            pltpu.VMEM((WIDTH + 16, KEYS), jnp.bfloat16),
            pltpu.VMEM((SHARD, WIDTH), jnp.bfloat16),
            pltpu.VMEM((LANDED, WIDTH), jnp.bfloat16),
            pltpu.VMEM((SHARD // 2 * GROUP, WIDTH), jnp.bfloat16),
            pltpu.VMEM((2, KEYS, WIDTH), jnp.bfloat16),
            pltpu.VMEM((4, BLOCK, GROUP * WIDTH), jnp.bfloat16),
            pltpu.VMEM((ROWS, WIDTH), jnp.float32),
            pltpu.SemaphoreType.DMA((4,)),
            pltpu.SemaphoreType.DMA((2 * BACK + 1, ITEMS)),
            pltpu.SemaphoreType.DMA((BACK + 1, ITEMS)),
            pltpu.SemaphoreType.DMA((3, PIECES)),
            pltpu.SemaphoreType.DMA((3, PIECES)),
            pltpu.SemaphoreType.DMA((PIECES,)),
        ],
        compiler_params=pltpu.CompilerParams(
            collective_id=0, has_side_effects=True, vmem_limit_bytes=56 << 20
        ),
        cost_estimate=pl.CostEstimate(
            flops=4 * SHARD * GROUP * KEYS * WIDTH, bytes_accessed=4 << 20, transcendentals=SHARD * GROUP * KEYS
        ),
    )(
        queries.reshape(SHARD * GROUP, WIDTH),
        keys.reshape(SHARD, WIDTH),
        values.reshape(SHARD, WIDTH),
        doc_ids.reshape(2, WIDTH),
    )


def solution(mesh):
    return jax.shard_map(
        body,
        mesh=mesh,
        in_specs=(P("ctx", "kvh", None), P("ctx", "kvh", None), P("ctx", "kvh", None), P("ctx")),
        out_specs=P(("ctx", "kvh"), None),
        check_vma=False,
    )
```

```python
import functools

import jax
import jax.numpy as jnp
from jax import lax
from jax.experimental import pallas as pl
from jax.experimental.pallas import tpu as pltpu
from jax.sharding import PartitionSpec as P

MESH = pl.DeviceIdType.MESH
BACK = 3
RING = 4
CROSS = [(y, by) for y in range(RING) for by in range(1, BACK + 1) if y + by >= RING]
DIRECT = ([(1, 3), (2, 2), (2, 3), (3, 1)], [(1, 3), (2, 2), (2, 3), (3, 2)])
PASSED = [[flow for flow in CROSS if flow not in straight] for straight in DIRECT]
SHARD = 256
LANDED = SHARD + 16
ITEMS = 2
GROUP = 16
WIDTH = 128
KEYS = (BACK + 1) * SHARD
BLOCK = 64
WINDOW = BACK * SHARD + 2 * BLOCK
TILE = 32
PIECES = BLOCK // TILE
ROWS = TILE * GROUP
HIDE = -131072.0
EXP2 = 1.4426950408889634 / WIDTH**0.5
LAST = (((1,), (1,)), ((), ()))
PLAIN = (((1,), (0,)), ((), ()))


def kernel(
    q_hbm, k_hbm, v_hbm, ids_hbm, out_hbm,
    q_buf, k_buf, v_buf, own_ids, vt_buf, k_pass, v_pass, pick, bias, stage, turned,
    load_sem, kv_send, kv_recv, out_send, out_recv, own_sem,
):
    ctx = lax.axis_index("ctx")
    kvh = lax.axis_index("kvh")
    shards = lax.axis_size("ctx")
    pair, core = kvh // 2, kvh % 2

    ring, place = ctx // RING, ctx % RING
    rings = shards // RING

    def any_of(conditions):
        return functools.reduce(jnp.logical_or, conditions, False)

    def sends(flows, by=None):
        found = [(ring % 2 == i) & (place == y) for i in range(2) for y in sorted({y for y, b in flows[i] if by in (None, b)})]
        return (ring < rings - 1) & any_of(found)

    def after(flows, by=None, end=False):
        found = [
            (ring % 2 == 1 - i) & (place == y)
            for i in range(2)
            for y in sorted({y + (b - RING) * end for y, b in flows[i] if by in (None, b)})
        ]
        return (ring >= 1) & any_of(found)

    steps = range(1, BACK + 1)
    gives, takes = sends(PASSED), after(PASSED)
    straight = {by: (place + by < RING) | sends(DIRECT, by) for by in steps}
    reached = {by: (place >= by) | after(DIRECT, by, end=True) for by in steps}
    onward = {by: after(PASSED, by) for by in steps}
    fed = {by: after(PASSED, by, end=True) for by in steps}

    def owner(step):
        late, odd = step // 2, step % 2
        x = (1 - pair) * (1 - late) + pair * late
        c = (1 - odd) * (1 - late) + late * ((1 - core) * (1 - odd) + core * odd)
        return 2 * x + c

    barrier = pltpu.get_barrier_semaphore()
    for step in range(3):
        pl.semaphore_signal(barrier, inc=1, device_id=(ctx, owner(step)), device_id_type=MESH)

    for by in range(1, BACK + 1):

        @pl.when(reached[by])
        def _():
            pl.semaphore_signal(barrier, inc=1, device_id=(ctx - by, kvh), device_id_type=MESH)

        @pl.when(fed[by])
        def _():
            pl.semaphore_signal(barrier, inc=1, device_id=(ctx - by + RING, kvh), device_id_type=MESH)

    @pl.when(takes)
    def _():
        pl.semaphore_signal(barrier, inc=1, device_id=(ctx - RING, kvh), device_id_type=MESH)

    own = BACK * SHARD
    loads = [
        pltpu.make_async_copy(ids_hbm, own_ids, load_sem.at[0]),
        pltpu.make_async_copy(k_hbm, k_buf.at[pl.ds(own, SHARD)], load_sem.at[1]),
        pltpu.make_async_copy(v_hbm, v_buf.at[BACK, pl.ds(0, SHARD)], load_sem.at[2]),
        pltpu.make_async_copy(q_hbm, q_buf, load_sem.at[3]),
    ]
    for load in loads:
        load.start()

    for load in loads[:3]:
        load.wait()
    ids = jnp.concatenate([own_ids[...].astype(jnp.float32), jnp.zeros((14, WIDTH), jnp.float32)], axis=0)
    v_buf[BACK, SHARD:, :] = ids.astype(jnp.bfloat16)

    sent_to = [gives, *straight.values(), *onward.values()]
    pl.semaphore_wait(barrier, 3 + sum(to.astype(jnp.int32) for to in sent_to))

    def part_rows(to, first=0, count=SHARD):
        return pl.ds(pl.multiple_of(to * SHARD + first, WIDTH), count)

    def part(i, to):
        if isinstance(to, int) and to == BACK + 1:
            return (v_pass, k_pass)[i]
        return v_buf.at[to] if i == 0 else k_buf.at[part_rows(to)]

    def move(i, to, target, passed):
        src = part(i, BACK)
        slot = BACK if isinstance(to, int) and to > BACK else to
        if passed:
            src = part(i, BACK + 1)
        return pltpu.make_async_remote_copy(
            src_ref=src, dst_ref=part(i, to),
            send_sem=kv_send.at[slot + (BACK + 1) * passed, i], recv_sem=kv_recv.at[slot, i],
            device_id=(target, kvh), device_id_type=MESH,
        )

    @pl.when(gives)
    def _():
        for i in range(ITEMS):
            move(i, BACK + 1, ctx + RING, False).start()

    @pl.when(straight[1])
    def _():
        for i in range(ITEMS):
            move(i, BACK - 1, ctx + 1, False).start()

    for i in range(ITEMS):
        for by in (2, 3):

            @pl.when(straight[by])
            def _():
                move(i, BACK - by, ctx + by, False).start()

    for by in range(1, BACK + 1):

        @pl.when(ctx < by)
        def _():
            rows = pl.ds((BACK - by) * SHARD, SHARD)
            k_buf[rows] = jnp.zeros((SHARD, WIDTH), jnp.bfloat16)
            v_buf[BACK - by, :SHARD, :] = jnp.zeros((SHARD, WIDTH), jnp.bfloat16)
            v_buf[BACK - by, SHARD:, :] = jnp.full((16, WIDTH), -1, jnp.bfloat16)

    token = lax.broadcasted_iota(jnp.int32, (SHARD // 2 * GROUP, WIDTH), 0) // GROUP
    lane = lax.broadcasted_iota(jnp.int32, (SHARD // 2 * GROUP, WIDTH), 1)
    pick[...] = jnp.where(token == lane, 1.0, 0.0).astype(jnp.bfloat16)

    def hide(to, causal=False):
        key_ids = v_buf[to, SHARD:, :].astype(jnp.float32)
        query_ids = v_buf[BACK, SHARD:, :].astype(jnp.float32)
        for r in range(2):
            column = jnp.broadcast_to(key_ids[r : r + 1], (WIDTH, WIDTH)).T
            key_pos = lax.broadcasted_iota(jnp.int32, (WIDTH, WIDTH), 0) + r * WIDTH
            query_pos = lax.broadcasted_iota(jnp.int32, (WIDTH, WIDTH), 1)
            for half in range(2):
                seen = column == query_ids[half : half + 1]
                if causal:
                    seen = seen & (key_pos <= query_pos + half * WIDTH)
                rows = part_rows(to, r * WIDTH, WIDTH)
                bias[half, rows, :] = jnp.where(seen, 0.0, HIDE).astype(jnp.bfloat16)

    def turn(to):
        vt_buf[:WIDTH, part_rows(to)] = v_buf[to, :SHARD, :].T

    def arrived(to, items):
        @pl.when(ctx >= BACK - to)
        def _():
            for i in items:
                move(i, to, ctx, False).wait_recv()

    vt_buf[WIDTH:, :] = jnp.ones((16, KEYS), jnp.bfloat16)
    loads[3].wait()
    hide(BACK, causal=True)
    turn(BACK)

    @pl.when(takes)
    def _():
        for i in range(ITEMS):
            move(i, BACK + 1, ctx, False).wait_recv()
            for by in range(1, BACK + 1):

                @pl.when(onward[by])
                def _():
                    move(i, BACK - by, ctx + by - RING, True).start()

    def outgoing(step, piece):
        rows = pl.ds(pl.multiple_of(piece * TILE, TILE), TILE)
        slot = core * (1 - step // 2) + 2 * (step // 2)
        return pltpu.make_async_remote_copy(
            src_ref=stage.at[step, rows],
            dst_ref=out_hbm.at[rows, pl.ds(pl.multiple_of(kvh * GROUP * WIDTH, WIDTH), GROUP * WIDTH)],
            send_sem=out_send.at[step, piece], recv_sem=out_recv.at[slot, piece],
            device_id=(ctx, owner(step)), device_id_type=MESH,
        )

    def kept(piece):
        rows = pl.ds(pl.multiple_of(piece * TILE, TILE), TILE)
        return pltpu.make_async_copy(
            stage.at[3, rows],
            out_hbm.at[rows, pl.ds(pl.multiple_of(kvh * GROUP * WIDTH, WIDTH), GROUP * WIDTH)],
            own_sem.at[piece],
        )

    def asked(step, piece):
        block = owner(step)
        first = pl.multiple_of((block * PIECES + piece) * ROWS, ROWS)
        inside = pl.multiple_of(((block % 2) * PIECES + piece) * ROWS, ROWS)
        return jnp.concatenate([q_buf[pl.ds(first, ROWS), :], pick[pl.ds(inside, ROWS), :]], axis=1)

    def scores(keys, queries):
        return lax.dot_general(keys, queries, LAST, preferred_element_type=jnp.float32)

    def weighed(values, score, top):
        weight = jnp.exp2((score - top) * EXP2).astype(jnp.bfloat16)
        return lax.dot_general(values, weight, PLAIN, preferred_element_type=jnp.float32)

    def finish(step, piece, summed):
        turned[...] = (summed[:WIDTH] / summed[WIDTH : WIDTH + 1]).T
        tokens = pl.ds(pl.multiple_of(piece * TILE, TILE), TILE)
        for head in range(GROUP):
            stage[step, tokens, head * WIDTH : (head + 1) * WIDTH] = turned[
                pl.ds(head, TILE, stride=GROUP), :
            ].astype(jnp.bfloat16)

    late = (BACK - 1 - place) * (1 - place // BACK)
    early = [1 - (late + 1) // 2, 2 - late // 2, BACK]
    for to in early[:2]:
        arrived(to, range(ITEMS))
        hide(to)
        turn(to)
    half = owner(0) // 2
    queries = asked(0, 0)

    def keys_of(to):
        return jnp.concatenate([k_buf[part_rows(to), :], bias[half, part_rows(to), :]], axis=1)

    score = scores(jnp.concatenate([keys_of(to) for to in early], axis=0), queries)
    early_top = jnp.max(score, axis=0, keepdims=True)
    early_sum = weighed(jnp.concatenate([vt_buf[:, part_rows(to)] for to in early], axis=1), score, early_top)
    arrived(late, [0])
    hide(late)
    turn(late)
    arrived(late, [1])
    score = scores(keys_of(late), queries)
    top = jnp.maximum(early_top, jnp.max(score, axis=0, keepdims=True))
    late_sum = weighed(vt_buf[:, part_rows(late)], score, top)
    finish(0, 0, early_sum * jnp.exp2((early_top - top) * EXP2) + late_sum)
    outgoing(0, 0).start()

    def work(i, _):
        step, piece = i // PIECES, i % PIECES
        block = owner(step)
        window = pl.ds(pl.multiple_of(block // 2 * WIDTH, WIDTH), WINDOW)
        score = scores(jnp.concatenate([k_buf[window, :], bias[block // 2, window, :]], axis=1), asked(step, piece))
        top = jnp.max(score, axis=0, keepdims=True)
        finish(step, piece, weighed(vt_buf[:, window], score, top))

        @pl.when(step < 3)
        def _():
            outgoing(step, piece).start()

        @pl.when(step == 3)
        def _():
            kept(piece).start()

        return 0

    lax.fori_loop(1, 4 * PIECES, work, 0)

    for i in range(ITEMS):
        for by in range(1, BACK + 1):

            @pl.when(straight[by])
            def _():
                move(i, BACK - by, ctx, False).wait_send()

            @pl.when(onward[by])
            def _():
                move(i, BACK - by, ctx, True).wait_send()

        @pl.when(gives)
        def _():
            move(i, BACK + 1, ctx, False).wait_send()

    for piece in range(PIECES):
        kept(piece).wait()
        for step in range(3):
            outgoing(step, piece).wait_send()
        for slot in range(3):
            rows = pl.ds(piece * TILE, TILE)
            pltpu.make_async_remote_copy(
                src_ref=stage.at[slot, rows], dst_ref=out_hbm.at[rows, pl.ds(0, GROUP * WIDTH)],
                send_sem=out_send.at[slot, piece], recv_sem=out_recv.at[slot, piece],
                device_id=(ctx, owner(0)), device_id_type=MESH,
            ).wait_recv()


def body(queries, keys, values, doc_ids):
    anywhere = pl.BlockSpec(memory_space=pl.ANY)
    return pl.pallas_call(
        kernel,
        name="attend",
        out_shape=pltpu.VMEM((BLOCK, 4 * GROUP * WIDTH), jnp.bfloat16),
        in_specs=[anywhere] * 4,
        out_specs=pl.BlockSpec(memory_space=pltpu.VMEM),
        scratch_shapes=[
            pltpu.VMEM((SHARD * GROUP, WIDTH), jnp.bfloat16),
            pltpu.VMEM((KEYS, WIDTH), jnp.bfloat16),
            pltpu.VMEM((BACK + 1, LANDED, WIDTH), jnp.bfloat16),
            pltpu.VMEM((2, WIDTH), jnp.int32),
            pltpu.VMEM((WIDTH + 16, KEYS), jnp.bfloat16),
            pltpu.VMEM((SHARD, WIDTH), jnp.bfloat16),
            pltpu.VMEM((LANDED, WIDTH), jnp.bfloat16),
            pltpu.VMEM((SHARD // 2 * GROUP, WIDTH), jnp.bfloat16),
            pltpu.VMEM((2, KEYS, WIDTH), jnp.bfloat16),
            pltpu.VMEM((4, BLOCK, GROUP * WIDTH), jnp.bfloat16),
            pltpu.VMEM((ROWS, WIDTH), jnp.float32),
            pltpu.SemaphoreType.DMA((4,)),
            pltpu.SemaphoreType.DMA((2 * BACK + 1, ITEMS)),
            pltpu.SemaphoreType.DMA((BACK + 1, ITEMS)),
            pltpu.SemaphoreType.DMA((3, PIECES)),
            pltpu.SemaphoreType.DMA((3, PIECES)),
            pltpu.SemaphoreType.DMA((PIECES,)),
        ],
        compiler_params=pltpu.CompilerParams(
            collective_id=0, has_side_effects=True, vmem_limit_bytes=56 << 20
        ),
        cost_estimate=pl.CostEstimate(
            flops=4 * SHARD * GROUP * KEYS * WIDTH, bytes_accessed=4 << 20, transcendentals=SHARD * GROUP * KEYS
        ),
    )(
        queries.reshape(SHARD * GROUP, WIDTH),
        keys.reshape(SHARD, WIDTH),
        values.reshape(SHARD, WIDTH),
        doc_ids.reshape(2, WIDTH),
    )


def solution(mesh):
    return jax.shard_map(
        body,
        mesh=mesh,
        in_specs=(P("ctx", "kvh", None), P("ctx", "kvh", None), P("ctx", "kvh", None), P("ctx")),
        out_specs=P(("ctx", "kvh"), None),
        check_vma=False,
    )
```
